32 devices in a mesh: section: 2 (over core), group: 16 (over z, y, x).
Axes of the slice: x: 2, y: 2, z: 4, core: 2. Of those that a mesh axis runs over, the one named last changes fastest.
Arguments:
- upstream: bfloat16 [2, 256, 8192], P('section', None, 'group'), may hold values from -6 to 6
- projected: bfloat16 [2, 3, 256, 3, 4096], P('section', None, None, None, 'group'), may hold values from -6 to 6
- w_in: bfloat16 [2, 8192, 3, 4096], P('section', None, None, 'group'), may hold values from -0.0546875 to 0.0546875
- w_out: bfloat16 [2, 4096, 8192], P('section', 'group'), may hold values from -0.0625 to 0.0625
- short_filter: float32 [2, 3, 7, 4096], P('section', None, None, 'group'), may hold values from -2 to 2
- long_filter: float32 [2, 128, 4096], P('section', None, 'group'), may hold values from -0.5 to 0.5
Outputs:
- input_grad: bfloat16 [2, 256, 8192], P('section', None, 'group')
- proj_grad: bfloat16 [2, 3, 256, 3, 4096], P('section', None, None, None, 'group')
- long_filter_grad: float32 [2, 128, 4096], P('section', None, 'group')
- short_filter_grad: float32 [2, 3, 7, 4096], P('section', None, None, 'group')
The draws below stay inside these ranges and needn't reach their ends.
All inputs are finite; a program needn't handle non-finite values.
Results may differ from the reference program's by a relative error of at most 0.033.
Values may be sent and summed in bfloat16 or wider, within the bound.
A program may use at most 128 MiB of HBM per device.

```python
import jax
import jax.numpy as jnp
from jax import lax

D = 8192
C = 4096
TOK = 256
MIXERS = 3
SW = 7
LW = 128
N_SECTION = 2
N_GROUP = 16


def block_scale(rng, shape, split, least, largest):
    level = 1.0
    for axis_at, shards_of in split:
        steps = jax.random.uniform(jax.random.fold_in(jax.random.fold_in(rng, 6), axis_at), (shards_of,), jnp.float32, least / len(split), largest / len(split))
        level = level * jnp.repeat(jnp.exp(steps), shape[axis_at] // shards_of).reshape((-1,) + (1,) * (len(shape) - 1 - axis_at))
    return level


def noise(own_key, shape, spread, bound, shards=(), kind=jnp.bfloat16):
    drawn = spread * jax.random.normal(own_key, shape, jnp.float32)
    if shards:
        drawn = drawn * block_scale(own_key, shape, shards, -0.22, 0.18)
    return jnp.clip(drawn, -bound, bound).astype(kind)


def setup_inputs(seed: int = 0) -> dict:
    key_of = jax.random.split(jax.random.key(seed), 7)
    upstream = noise(key_of[0], (N_SECTION, TOK, D), 1.0, 6.0, ((0, 2), (2, 16)))
    projected = noise(key_of[1], (N_SECTION, MIXERS, TOK, 3, C), 1.0, 6.0, ((0, 2), (4, 16)))
    w_in = noise(key_of[2], (N_SECTION, D, 3, C), (3 * C) ** -0.5, 0.0546875, ((0, 2), (3, 16)))
    w_out = noise(key_of[3], (N_SECTION, C, D), D ** -0.5, 0.0625, ((0, 2), (1, 16)))
    short_filter = noise(key_of[4], (N_SECTION, 3, SW, C), SW ** -0.5, 2.0, ((0, 2), (3, 16)), jnp.float32)
    long_filter = noise(key_of[5], (N_SECTION, LW, C), LW ** -0.5, 0.5, ((0, 2), (2, 16)), jnp.float32)
    return dict(upstream=upstream, projected=projected, w_in=w_in, w_out=w_out, short_filter=short_filter, long_filter=long_filter)


def causal(signal, filter_taps):
    extent = filter_taps.shape[0]
    length = signal.shape[0]
    padded = jnp.pad(signal, ((extent - 1, 0), (0, 0)))

    def add_tap(step, running):
        index = jnp.asarray(step).astype(jnp.int32)
        piece = lax.dynamic_slice_in_dim(padded, (extent - 1 - index).astype(jnp.int32), length, 0)
        weight = lax.dynamic_index_in_dim(filter_taps, index, 0, keepdims=False)
        return running + weight[None, :] * piece
    return lax.fori_loop(0, extent, add_tap, jnp.zeros(signal.shape, signal.dtype))

def anticausal(gradient, filter_taps):
    extent = filter_taps.shape[0]
    length = gradient.shape[0]
    padded = jnp.pad(gradient, ((0, extent - 1), (0, 0)))

    def add_tap(step, running):
        index = jnp.asarray(step).astype(jnp.int32)
        piece = lax.dynamic_slice_in_dim(padded, index, length, 0)
        weight = lax.dynamic_index_in_dim(filter_taps, index, 0, keepdims=False)
        return running + weight[None, :] * piece
    return lax.fori_loop(0, extent, add_tap, jnp.zeros(gradient.shape, gradient.dtype))

def tap_grad(gradient, signal, extent):
    length = signal.shape[0]
    padded = jnp.pad(signal, ((extent - 1, 0), (0, 0)))

    def one_tap(index):
        piece = lax.dynamic_slice_in_dim(padded, (extent - 1 - index).astype(jnp.int32), length, 0)
        return lax.optimization_barrier(jnp.sum(gradient * piece, axis=0))
    return lax.map(one_tap, jnp.arange(extent, dtype=jnp.int32))

def mixer_backward(out_grad, projected_rows, short_taps, long_taps):
    signal = projected_rows.astype(jnp.float32)
    query_conv = causal(signal[:, 0], short_taps[0])
    key_conv = causal(signal[:, 1], short_taps[1])
    value_conv = causal(signal[:, 2], short_taps[2])
    gating = key_conv * value_conv
    long_mixed = causal(gating, long_taps)
    mixed_grad = out_grad * query_conv
    query_grad = out_grad * long_mixed
    gating_grad = anticausal(mixed_grad, long_taps)
    key_grad = gating_grad * value_conv
    value_grad = gating_grad * key_conv
    proj_grad = jnp.stack([anticausal(query_grad, short_taps[0]), anticausal(key_grad, short_taps[1]), anticausal(value_grad, short_taps[2])], axis=1).astype(jnp.bfloat16)
    long_grad = tap_grad(mixed_grad, gating, long_taps.shape[0])
    short_extent = short_taps.shape[1]
    short_grad = jnp.stack([tap_grad(query_grad, signal[:, 0], short_extent), tap_grad(key_grad, signal[:, 1], short_extent), tap_grad(value_grad, signal[:, 2], short_extent)], axis=0)
    return (proj_grad, long_grad, short_grad)

def block_sum(proj_grad, w_in_section):
    block_width = C // N_GROUP
    grad_blocks = proj_grad.reshape(TOK, 3, N_GROUP, block_width).transpose(2, 0, 1, 3).reshape(N_GROUP, TOK, 3 * block_width)
    weight_blocks = w_in_section.reshape(D, 3, N_GROUP, block_width).transpose(2, 0, 1, 3).reshape(N_GROUP, D, 3 * block_width)

    def add_block(running, operands):
        block_part = lax.dot_general(operands[0], operands[1], (((1,), (1,)), ((), ())), preferred_element_type=jnp.float32)
        rounded = lax.optimization_barrier(block_part.astype(jnp.bfloat16))
        return (running + rounded.astype(jnp.float32), None)
    running, _ = lax.scan(add_block, jnp.zeros((TOK, D), jnp.float32), (grad_blocks, weight_blocks))
    return running.astype(jnp.bfloat16)

def reference(upstream, projected, w_in, w_out, short_filter, long_filter):
    incoming = upstream
    grad_list = [[] for section_index in range(N_SECTION)]
    long_total = [jnp.zeros((LW, C), jnp.float32) for section_index in range(N_SECTION)]
    short_total = [jnp.zeros((3, SW, C), jnp.float32) for section_index in range(N_SECTION)]
    for round_index in range(MIXERS):
        outgoing_list = []
        for section_index in range(N_SECTION):
            out_grad = lax.dot_general(incoming[section_index], w_out[section_index], (((1,), (1,)), ((), ())), preferred_element_type=jnp.float32)
            proj_grad, long_grad, short_grad = mixer_backward(out_grad, projected[section_index, round_index], short_filter[section_index], long_filter[section_index])
            grad_list[section_index].append(proj_grad)
            long_total[section_index] = long_total[section_index] + long_grad
            short_total[section_index] = short_total[section_index] + short_grad
            outgoing_list.append(block_sum(proj_grad, w_in[section_index]))
        incoming = jnp.roll(jnp.stack(outgoing_list), -1, axis=0)
    proj_out = jnp.stack([jnp.stack(grad_list[section_index]) for section_index in range(N_SECTION)])
    return (incoming, proj_out, jnp.stack(long_total), jnp.stack(short_total))
```

```python
import functools

import jax
import jax.numpy as jnp
from jax import lax
from jax.experimental import pallas as pl
from jax.experimental.pallas import tpu as pltpu
from jax.sharding import PartitionSpec as P

HIGHEST = lax.Precision.HIGHEST


def depthwise(operand, kernel):
    result = lax.conv_general_dilated(
        operand[None],
        kernel[:, None, :],
        (1,),
        "VALID",
        dimension_numbers=("NWC", "WIO", "NWC"),
        feature_group_count=operand.shape[1],
        precision=HIGHEST,
    )
    return result[0]


def causal(signal, filter_taps):
    extent = filter_taps.shape[0]
    padded = jnp.pad(signal, ((extent - 1, 0), (0, 0)))
    return depthwise(padded, filter_taps[::-1])


def anticausal(gradient, filter_taps):
    extent = filter_taps.shape[0]
    padded = jnp.pad(gradient, ((0, extent - 1), (0, 0)))
    return depthwise(padded, filter_taps)


def tap_grad(gradient, signal, extent):
    padded = jnp.pad(signal, ((extent - 1, 0), (0, 0)))
    return depthwise(padded, gradient)[::-1]


def mixer_backward(out_grad, projected_rows, short_taps, long_taps):
    signal = projected_rows.astype(jnp.float32)
    query_conv = causal(signal[:, 0], short_taps[0])
    key_conv = causal(signal[:, 1], short_taps[1])
    value_conv = causal(signal[:, 2], short_taps[2])
    gating = key_conv * value_conv
    long_mixed = causal(gating, long_taps)
    mixed_grad = out_grad * query_conv
    query_grad = out_grad * long_mixed
    gating_grad = anticausal(mixed_grad, long_taps)
    key_grad = gating_grad * value_conv
    value_grad = gating_grad * key_conv
    proj_grad = jnp.stack(
        [
            anticausal(query_grad, short_taps[0]),
            anticausal(key_grad, short_taps[1]),
            anticausal(value_grad, short_taps[2]),
        ],
        axis=1,
    ).astype(jnp.bfloat16)
    long_grad = tap_grad(mixed_grad, gating, long_taps.shape[0])
    short_extent = short_taps.shape[1]
    short_grad = jnp.stack(
        [
            tap_grad(query_grad, signal[:, 0], short_extent),
            tap_grad(key_grad, signal[:, 1], short_extent),
            tap_grad(value_grad, signal[:, 2], short_extent),
        ],
        axis=0,
    )
    return (proj_grad, long_grad, short_grad)


NT = (((1,), (1,)), ((), ()))


def exchange_body(has_sum, has_gather, line, sections, *refs):
    refs = list(refs)
    take = lambda count: [refs.pop(0) for _ in range(count)]
    if has_sum:
        grad_ref, w_in_ref = take(2)
    else:
        (first_ref,) = take(1)
    if has_gather:
        (w_out_ref,) = take(1)
    (result_ref,) = take(1)
    if has_sum:
        part, got_p, got_q, got_up, got_down = take(5)
        p_send, p_recv, q_send, q_recv, up_send, up_recv, down_send, down_recv, turn_send, turn_recv = take(10)
    landed, = take(1)
    if has_gather:
        total, = take(1)
        gl_up, gl_down, gl_recv, gq_send, gq_recv, gp_send, gp_recv = take(7)
    section = lax.axis_index("section")
    me = lax.axis_index("group")
    a = me // 4
    y = (me // 2) % 2
    x = me % 2
    half_rows = landed.shape[1] // 2

    def block(t, yy, xx):
        return t * 4 + yy * 2 + xx

    to_x = {"group": block(a, y, 1 - x)}
    to_y = {"group": block(a, 1 - y, x)}
    above = {"group": lax.rem(me + 4, 4 * line)}
    below = {"group": lax.rem(me + 4 * line - 4, 4 * line)}
    to_section = {"section": lax.rem(section + sections - 1, sections)}
    from_section = {"section": lax.rem(section + 1, sections)}
    not_top = a < line - 1
    not_bottom = a > 0

    barrier = pltpu.get_barrier_semaphore()

    def greet(device):
        pl.semaphore_signal(barrier, inc=1, device_id=device, device_id_type=pl.DeviceIdType.MESH)

    greet(to_x)
    greet(to_y)
    pl.when(not_top)(lambda: greet(above))
    pl.when(not_bottom)(lambda: greet(below))
    if has_sum:
        greet(from_section)
    ends = 2 + jnp.where(not_top, 1, 0) + jnp.where(not_bottom, 1, 0)
    pl.semaphore_wait(barrier, ends + (1 if has_sum else 0))

    def far_first(k):
        low = line - 1 - k
        low = jnp.where(low <= a, low - 1, low)
        high = jnp.where(k >= a, k + 1, k)
        other = jnp.where(a < line // 2, low, high)
        return jnp.where(k == line - 1, a, other)

    def near_first(k):
        return far_first(line - 1 - k)

    def rows(half):
        return pl.ds(half * half_rows, half_rows)

    def copy(source, target, send, recv, device):
        return pltpu.make_async_remote_copy(
            src_ref=source,
            dst_ref=target,
            send_sem=send,
            recv_sem=recv,
            device_id=device,
            device_id_type=pl.DeviceIdType.MESH,
        )

    def sides(half):
        if half == 0:
            return y, x, to_y, to_x, lambda t, pp, qq: block(t, pp, qq)
        return x, y, to_x, to_y, lambda t, pp, qq: block(t, qq, pp)

    if has_sum:
        width = part.shape[2]

        def p_copy(half, t, qq):
            p, q, p_dev, q_dev, at = sides(half)
            slot = t * 2 + qq
            return copy(
                part.at[at(t, 1 - p, qq), rows(half)],
                got_p.at[half, slot],
                p_send.at[half, slot],
                p_recv.at[half, slot],
                p_dev,
            )

        def q_copy(half, t):
            p, q, p_dev, q_dev, at = sides(half)
            return copy(
                part.at[at(t, p, 1 - q), rows(half)],
                got_q.at[half, t],
                q_send.at[half, t],
                q_recv.at[half, t],
                q_dev,
            )

        def up_copy(half, t):
            return copy(
                part.at[block(t, y, x), rows(half)], got_up.at[half, t], up_send.at[half, t], up_recv.at[half, t], above
            )

        def down_copy(half, t):
            return copy(
                part.at[block(t, y, x), rows(half)],
                got_down.at[half, t],
                down_send.at[half, t],
                down_recv.at[half, t],
                below,
            )

        def turn_copy(half):
            target = landed.at[me, rows(half)] if has_gather else landed.at[0, rows(half)]
            return copy(part.at[me, rows(half)], target, turn_send.at[half], turn_recv.at[half], to_section)

        def product(b):
            w_rows = pl.ds(pl.multiple_of(b * width, width), width)
            value = lax.dot_general(grad_ref[0], w_in_ref[0, w_rows, :], NT, preferred_element_type=jnp.float32)
            for i in range(1, 3):
                value += lax.dot_general(grad_ref[i], w_in_ref[i, w_rows, :], NT, preferred_element_type=jnp.float32)
            part[b] = value.astype(part.dtype)

        def first_step(k, carry):
            t = far_first(k)
            product(block(t, 1 - y, 1 - x))
            p_copy(0, t, 1 - x).start()
            p_copy(1, t, 1 - y).start()
            product(block(t, 1 - y, x))
            p_copy(0, t, x).start()
            product(block(t, y, 1 - x))
            p_copy(1, t, y).start()
            product(block(t, y, x))
            return carry

        lax.fori_loop(0, line, first_step, 0)

        def second_step(k, carry):
            t = far_first(k)
            for half in range(2):
                p, q, p_dev, q_dev, at = sides(half)
                p_copy(half, t, 1 - q).wait_recv()
                b = at(t, p, 1 - q)
                value = part[b, rows(half)].astype(jnp.float32) + got_p[half, t * 2 + 1 - q].astype(jnp.float32)
                part[b, rows(half)] = value.astype(part.dtype)
                q_copy(half, t).start()
            return carry

        lax.fori_loop(0, line, second_step, 0)

        def third_step(k, carry):
            t = far_first(k)
            for half in range(2):
                p, q, p_dev, q_dev, at = sides(half)
                p_copy(half, t, q).wait_recv()
                q_copy(half, t).wait_recv()
                b = block(t, y, x)
                total_ref = sum_ref.at[half]
                total_ref[...] = (
                    part[b, rows(half)].astype(jnp.float32)
                    + got_p[half, t * 2 + q].astype(jnp.float32)
                    + got_q[half, t].astype(jnp.float32)
                )

                @pl.when(jnp.logical_and(t >= a, not_bottom))
                def _():
                    up_copy(half, t).wait_recv()
                    total_ref[...] += got_up[half, t].astype(jnp.float32)

                @pl.when(jnp.logical_and(t <= a, not_top))
                def _():
                    down_copy(half, t).wait_recv()
                    total_ref[...] += got_down[half, t].astype(jnp.float32)

                part[b, rows(half)] = total_ref[...].astype(part.dtype)
                pl.when(t > a)(lambda: up_copy(half, t).start())
                pl.when(t < a)(lambda: down_copy(half, t).start())
                pl.when(t == a)(lambda: turn_copy(half).start())
            return carry

        (sum_ref,) = take(1)
        lax.fori_loop(0, line, third_step, 0)
    else:
        landed[me] = first_ref[...]

    if has_gather:
        depth = landed.shape[2]

        def gl_copy(half, t, send, device):
            piece = landed.at[block(t, y, x), rows(half)]
            return copy(piece, piece, send.at[half, t], gl_recv.at[half, t], device)

        def gq_copy(half, t, arriving):
            p, q, p_dev, q_dev, at = sides(half)
            piece = landed.at[at(t, p, 1 - q if arriving else q), rows(half)]
            return copy(piece, piece, gq_send.at[half, t], gq_recv.at[half, t], q_dev)

        def gp_copy(half, t, qq, arriving):
            p, q, p_dev, q_dev, at = sides(half)
            piece = landed.at[at(t, 1 - p if arriving else p, qq), rows(half)]
            slot = t * 2 + qq
            return copy(piece, piece, gp_send.at[half, slot], gp_recv.at[half, slot], p_dev)

        def add_block(b):
            columns = pl.ds(pl.multiple_of(b * depth, depth), depth)
            total[...] += lax.dot_general(landed[b], w_out_ref[:, columns], NT, preferred_element_type=jnp.float32)

        total[...] = jnp.zeros_like(total)

        def line_step(k, carry):
            t = near_first(k)
            for half in range(2):
                p, q, p_dev, q_dev, at = sides(half)
                if has_sum:
                    pl.when(t == a)(lambda: turn_copy(half).wait_recv())
                pl.when(t != a)(lambda: gl_copy(half, t, gl_up, above).wait_recv())
                pl.when(jnp.logical_and(t <= a, not_top))(lambda: gl_copy(half, t, gl_up, above).start())
                pl.when(jnp.logical_and(t >= a, not_bottom))(lambda: gl_copy(half, t, gl_down, below).start())
                gq_copy(half, t, False).start()
                gp_copy(half, t, q, False).start()
            add_block(block(t, y, x))
            return carry

        lax.fori_loop(0, line, line_step, 0)

        def pass_step(k, carry):
            t = near_first(k)
            for half in range(2):
                p, q, p_dev, q_dev, at = sides(half)
                gq_copy(half, t, True).wait_recv()
                gp_copy(half, t, 1 - q, False).start()
            return carry

        lax.fori_loop(0, line, pass_step, 0)

        def last_step(k, carry):
            t = near_first(k)
            gp_copy(0, t, x, True).wait_recv()
            add_block(block(t, 1 - y, x))
            gp_copy(1, t, y, True).wait_recv()
            add_block(block(t, y, 1 - x))
            gp_copy(0, t, 1 - x, True).wait_recv()
            gp_copy(1, t, 1 - y, True).wait_recv()
            add_block(block(t, 1 - y, 1 - x))
            return carry

        lax.fori_loop(0, line, last_step, 0)
        result_ref[...] = total[...]
    else:
        for half in range(2):
            turn_copy(half).wait_recv()
        result_ref[...] = landed[0]

    def settle(t, carry):
        for half in range(2):
            if has_sum:
                for qq in range(2):
                    p_copy(half, t, qq).wait_send()
                q_copy(half, t).wait_send()
                pl.when(t > a)(lambda: up_copy(half, t).wait_send())
                pl.when(t < a)(lambda: down_copy(half, t).wait_send())
            if has_gather:
                pl.when(jnp.logical_and(t <= a, not_top))(lambda: gl_copy(half, t, gl_up, above).wait_send())
                pl.when(jnp.logical_and(t >= a, not_bottom))(lambda: gl_copy(half, t, gl_down, below).wait_send())
                gq_copy(half, t, False).wait_send()
                for qq in range(2):
                    gp_copy(half, t, qq, False).wait_send()
        return carry

    lax.fori_loop(0, line, settle, 0)
    if has_sum:
        for half in range(2):
            turn_copy(half).wait_send()


def exchange(kind, *operands):
    has_sum = kind != "gather"
    has_gather = kind != "sum"
    group = lax.axis_size("group")
    sections = lax.axis_size("section")
    line = group // 4
    if has_sum:
        parts, tokens, _ = operands[0].shape
        width = operands[1].shape[1] // group
    else:
        tokens, width = operands[0].shape
    half_rows = tokens // 2
    dma = pltpu.SemaphoreType.DMA
    scratch = []
    piece = lambda *lead: pltpu.VMEM(lead + (half_rows, width), jnp.bfloat16)
    if has_sum:
        scratch += [pltpu.VMEM((group, tokens, width), jnp.bfloat16)]
        scratch += [piece(2, 2 * line), piece(2, line), piece(2, line), piece(2, line)]
        scratch += [dma((2, 2 * line))] * 2 + [dma((2, line))] * 6 + [dma((2,))] * 2
    scratch += [pltpu.VMEM((group if has_gather else 1, tokens, width), jnp.bfloat16)]
    if has_gather:
        local_ch = operands[-1].shape[0]
        scratch += [pltpu.VMEM((tokens, local_ch), jnp.float32)]
        scratch += [dma((2, line))] * 5 + [dma((2, 2 * line))] * 2
        out_shape = jax.ShapeDtypeStruct((tokens, local_ch), jnp.float32)
    else:
        out_shape = jax.ShapeDtypeStruct((tokens, width), jnp.bfloat16)
    if has_sum:
        scratch += [pltpu.VMEM((2, half_rows, width), jnp.float32)]
    return pl.pallas_call(
        functools.partial(exchange_body, has_sum, has_gather, line, sections),
        out_shape=out_shape,
        in_specs=[pl.BlockSpec(memory_space=pltpu.VMEM)] * len(operands),
        out_specs=pl.BlockSpec(memory_space=pltpu.VMEM),
        scratch_shapes=scratch,
        compiler_params=pltpu.CompilerParams(
            collective_id={"gather": 0, "both": 1, "sum": 2}[kind],
            has_side_effects=True,
            vmem_limit_bytes=48 * 2**20,
        ),
        name="exchange_" + kind,
    )(*operands)


def local(upstream, projected, w_in, w_out, short_filter, long_filter):
    rounds = projected.shape[1]
    in_parts = w_in[0].transpose(1, 0, 2)
    out_rows = w_out[0]
    short_taps = short_filter[0]
    long_taps = long_filter[0]
    grad_list = []
    long_total = jnp.zeros(long_taps.shape, jnp.float32)
    short_total = jnp.zeros(short_taps.shape, jnp.float32)
    out_grad = exchange("gather", upstream[0], out_rows)
    for round_index in range(rounds):
        proj_grad, long_grad, short_grad = mixer_backward(
            out_grad, projected[0, round_index], short_taps, long_taps
        )
        grad_list.append(proj_grad)
        long_total = long_total + long_grad
        short_total = short_total + short_grad
        grad_parts = proj_grad.transpose(1, 0, 2)
        if round_index < rounds - 1:
            out_grad = exchange("both", grad_parts, in_parts, out_rows)
        else:
            incoming = exchange("sum", grad_parts, in_parts)
    return (incoming[None], jnp.stack(grad_list)[None], long_total[None], short_total[None])

def solution(mesh):
    in_specs = (
        P("section", None, "group"),
        P("section", None, None, None, "group"),
        P("section", None, None, "group"),
        P("section", "group", None),
        P("section", None, None, "group"),
        P("section", None, "group"),
    )
    out_specs = (
        P("section", None, "group"),
        P("section", None, None, None, "group"),
        P("section", None, "group"),
        P("section", None, None, "group"),
    )
    return jax.shard_map(local, mesh=mesh, in_specs=in_specs, out_specs=out_specs, check_vma=False)
```

```python
import functools

import jax
import jax.numpy as jnp
from jax import lax
from jax.experimental import pallas as pl
from jax.experimental.pallas import tpu as pltpu
from jax.sharding import PartitionSpec as P

NT = (((1,), (1,)), ((), ()))


LANES = 128
PAD = 8


def mixers_body(
    line,
    sections,
    first_ref,
    projected_ref,
    w_in_any,
    w_out_any,
    short_ref,
    long_ref,
    result_ref,
    proj_ref,
    long_out,
    short_out,
    w_in_ref,
    w_out_ref,
    weight_sems,
    part,
    got_p,
    got_q,
    got_up,
    got_down,
    sum_ref,
    turned,
    landed,
    total,
    signal,
    conv,
    gating,
    mixed,
    mixed_grad,
    grads,
    long_part,
    short_part,
    p_send,
    p_recv,
    q_send,
    q_recv,
    up_send,
    up_recv,
    down_send,
    down_recv,
    turn_send,
    turn_recv,
    gl_up,
    gl_down,
    gl_recv,
    gq_send,
    gq_recv,
    gp_send,
    gp_recv,
):
    rounds = projected_ref.shape[0]
    tokens = landed.shape[1]
    tiles = conv.shape[1]
    extent = long_ref.shape[0]
    short_extent = short_ref.shape[1]
    chunk = extent // line
    strip = min(tokens, 128)
    w_out_copy = pltpu.make_async_copy(w_out_any, w_out_ref, weight_sems.at[0])
    w_in_copy = pltpu.make_async_copy(w_in_any, w_in_ref, weight_sems.at[1])
    w_out_copy.start()
    w_in_copy.start()
    section = lax.axis_index("section")
    me = lax.axis_index("group")
    a = me // 4
    y = (me // 2) % 2
    x = me % 2
    half_rows = landed.shape[1] // 2

    def block(t, yy, xx):
        return t * 4 + yy * 2 + xx

    to_x = {"group": block(a, y, 1 - x)}
    to_y = {"group": block(a, 1 - y, x)}
    above = {"group": lax.rem(me + 4, 4 * line)}
    below = {"group": lax.rem(me + 4 * line - 4, 4 * line)}
    to_section = {"section": lax.rem(section + sections - 1, sections)}
    from_section = {"section": lax.rem(section + 1, sections)}
    not_top = a < line - 1
    not_bottom = a > 0

    barrier = pltpu.get_barrier_semaphore()

    def greet(device):
        pl.semaphore_signal(barrier, inc=1, device_id=device, device_id_type=pl.DeviceIdType.MESH)

    greet(to_x)
    greet(to_y)
    pl.when(not_top)(lambda: greet(above))
    pl.when(not_bottom)(lambda: greet(below))
    greet(from_section)
    ends = 2 + jnp.where(not_top, 1, 0) + jnp.where(not_bottom, 1, 0)
    pl.semaphore_wait(barrier, ends + 1)

    def far_first(k):
        low = line - 1 - k
        low = jnp.where(low <= a, low - 1, low)
        high = jnp.where(k >= a, k + 1, k)
        other = jnp.where(a < line // 2, low, high)
        return jnp.where(k == line - 1, a, other)

    def near_first(k):
        return far_first(line - 1 - k)

    def rows(half):
        return pl.ds(half * half_rows, half_rows)

    def copy(source, target, send, recv, device):
        return pltpu.make_async_remote_copy(
            src_ref=source,
            dst_ref=target,
            send_sem=send,
            recv_sem=recv,
            device_id=device,
            device_id_type=pl.DeviceIdType.MESH,
        )

    def sides(half):
        if half == 0:
            return y, x, to_y, to_x, lambda t, pp, qq: block(t, pp, qq)
        return x, y, to_x, to_y, lambda t, pp, qq: block(t, qq, pp)

    width = part.shape[2]

    def p_copy(half, t, qq):
        p, q, p_dev, q_dev, at = sides(half)
        slot = t * 2 + qq
        return copy(
            part.at[at(t, 1 - p, qq), rows(half)],
            got_p.at[half, slot],
            p_send.at[half, slot],
            p_recv.at[half, slot],
            p_dev,
        )

    def q_copy(half, t):
        p, q, p_dev, q_dev, at = sides(half)
        return copy(
            part.at[at(t, p, 1 - q), rows(half)],
            got_q.at[half, t],
            q_send.at[half, t],
            q_recv.at[half, t],
            q_dev,
        )

    def up_copy(half, t):
        return copy(
            part.at[block(t, y, x), rows(half)], got_up.at[half, t], up_send.at[half, t], up_recv.at[half, t], above
        )

    def down_copy(half, t):
        return copy(
            part.at[block(t, y, x), rows(half)],
            got_down.at[half, t],
            down_send.at[half, t],
            down_recv.at[half, t],
            below,
        )

    def turn_copy(half, r):
        return copy(
            part.at[me, rows(half)], turned.at[r, rows(half)], turn_send.at[half, r], turn_recv.at[half, r], to_section
        )

    depth = landed.shape[2]

    def gl_copy(half, t, send, device):
        piece = landed.at[block(t, y, x), rows(half)]
        return copy(piece, piece, send.at[half, t], gl_recv.at[half, t], device)

    def gq_copy(half, t, arriving):
        p, q, p_dev, q_dev, at = sides(half)
        piece = landed.at[at(t, p, 1 - q if arriving else q), rows(half)]
        return copy(piece, piece, gq_send.at[half, t], gq_recv.at[half, t], q_dev)

    def gp_copy(half, t, qq, arriving):
        p, q, p_dev, q_dev, at = sides(half)
        piece = landed.at[at(t, 1 - p if arriving else p, qq), rows(half)]
        slot = t * 2 + qq
        return copy(piece, piece, gp_send.at[half, slot], gp_recv.at[half, slot], p_dev)

    def add_block(b):
        columns = pl.ds(pl.multiple_of(b * depth, depth), depth)
        total[...] += lax.dot_general(landed[b], w_out_ref[:, columns], NT, preferred_element_type=jnp.float32)


    def lanes(ct):
        return slice(ct * LANES, (ct + 1) * LANES)

    def short_convs(r):
        for ct in range(tiles):
            for i in range(3):
                signal[i, ct, PAD:] = projected_ref[r, i, :, lanes(ct)].astype(jnp.float32)
                value = short_ref[i, 0:1, lanes(ct)] * signal[i, ct, PAD:]
                for j in range(1, short_extent):
                    value += short_ref[i, j : j + 1, lanes(ct)] * signal[i, ct, PAD - j : PAD - j + tokens]
                conv[i, ct] = value
            gating[ct, extent:] = conv[1, ct] * conv[2, ct]
            mixed[ct] = jnp.zeros((tokens, LANES), jnp.float32)

    def tap_sum(source, ct, base, step, first, count, start):
        def eight(n, running):
            base_tap = pl.multiple_of(first + n * 8, 8)
            weights = long_ref[pl.ds(base_tap, 8), lanes(ct)]
            for jj in range(8):
                j = base_tap + jj
                running += weights[jj : jj + 1] * source[ct, pl.ds(base + step * j, strip)]
            return running

        return lax.fori_loop(0, count // 8, eight, start)

    def long_conv(k):
        for ct in range(tiles):
            for t0 in range(0, tokens, strip):
                mixed[ct, t0 : t0 + strip] = tap_sum(
                    gating, ct, extent + t0, -1, k * chunk, chunk, mixed[ct, t0 : t0 + strip]
                )

    def folded(value):
        return value.reshape(value.shape[0] // 8, 8, LANES).sum(axis=0)

    def long_taps_grad(k):
        for ct in range(tiles):
            for t0 in range(0, tokens, strip):
                fixed = mixed_grad[ct, t0 : t0 + strip]

                def four(n, carry):
                    for jj in range(4):
                        j = k * chunk + n * 4 + jj
                        long_part[ct, j] += folded(fixed * gating[ct, pl.ds(extent + t0 - j, strip)])
                    return carry

                lax.fori_loop(0, chunk // 4, four, 0)

    def short_taps_grad():
        for ct in range(tiles):
            for i in range(3):
                for j in range(short_extent):
                    short_part[i, j, ct] += folded(grads[i, ct, :tokens] * signal[i, ct, PAD - j : PAD - j + tokens])

    def mixer(r):
        for ct in range(tiles):
            out_grad = total[:, lanes(ct)]
            mixed_grad[ct, :tokens] = out_grad * conv[0, ct]
            grads[0, ct, :tokens] = out_grad * mixed[ct]
        for ct in range(tiles):
            for t0 in range(0, tokens, strip):
                span = slice(t0, t0 + strip)
                gating_grad = tap_sum(mixed_grad, ct, t0, 1, 0, extent, jnp.zeros((strip, LANES), jnp.float32))
                grads[1, ct, span] = gating_grad * conv[2, ct, span]
                grads[2, ct, span] = gating_grad * conv[1, ct, span]
        for ct in range(tiles):
            for i in range(3):
                value = short_ref[i, 0:1, lanes(ct)] * grads[i, ct, :tokens]
                for j in range(1, short_extent):
                    value += short_ref[i, j : j + 1, lanes(ct)] * grads[i, ct, j : j + tokens]
                proj_ref[r, i, :, lanes(ct)] = value.astype(proj_ref.dtype)

    signal[...] = jnp.zeros_like(signal)
    gating[...] = jnp.zeros_like(gating)
    mixed_grad[...] = jnp.zeros_like(mixed_grad)
    grads[...] = jnp.zeros_like(grads)
    long_part[...] = jnp.zeros_like(long_part)
    short_part[...] = jnp.zeros_like(short_part)
    turned[rounds] = first_ref[...]

    def settle_sum(r):
        def settle(t, carry):
            for half in range(2):
                for qq in range(2):
                    p_copy(half, t, qq).wait_send()
                q_copy(half, t).wait_send()
                pl.when(t > a)(lambda: up_copy(half, t).wait_send())
                pl.when(t < a)(lambda: down_copy(half, t).wait_send())
            return carry

        lax.fori_loop(0, line, settle, 0)
        for half in range(2):
            turn_copy(half, r).wait_send()

    def settle_gather(t, carry):
        for half in range(2):
            pl.when(jnp.logical_and(t <= a, not_top))(lambda: gl_copy(half, t, gl_up, above).wait_send())
            pl.when(jnp.logical_and(t >= a, not_bottom))(lambda: gl_copy(half, t, gl_down, below).wait_send())
            gq_copy(half, t, False).wait_send()
            for qq in range(2):
                gp_copy(half, t, qq, False).wait_send()
        return carry

    def one_round(r, round_carry):
        total[...] = jnp.zeros_like(total)

        def line_step(k, carry):
            t = near_first(k)
            for half in range(2):
                p, q, p_dev, q_dev, at = sides(half)

                @pl.when(t == a)
                def _():
                    pl.when(r > 0)(lambda: turn_copy(half, r - 1).wait_recv())
                    landed[me, rows(half)] = turned[jnp.where(r > 0, r - 1, rounds), rows(half)]

                pl.when(t != a)(lambda: gl_copy(half, t, gl_up, above).wait_recv())
                pl.when(jnp.logical_and(t <= a, not_top))(lambda: gl_copy(half, t, gl_up, above).start())
                pl.when(jnp.logical_and(t >= a, not_bottom))(lambda: gl_copy(half, t, gl_down, below).start())
                gq_copy(half, t, False).start()
                gp_copy(half, t, q, False).start()

            @pl.when(k == 0)
            def _():
                pl.when(r == 0)(lambda: w_out_copy.wait())
                short_convs(r)

            add_block(block(t, y, x))
            return carry

        lax.fori_loop(0, line, line_step, 0)
        pl.when(r > 0)(lambda: settle_sum(r - 1))

        def pass_step(k, carry):
            t = near_first(k)
            for half in range(2):
                p, q, p_dev, q_dev, at = sides(half)
                gq_copy(half, t, True).wait_recv()
                gp_copy(half, t, 1 - q, False).start()
            long_conv(k)
            return carry

        lax.fori_loop(0, line, pass_step, 0)

        def last_step(k, carry):
            t = near_first(k)
            gp_copy(0, t, x, True).wait_recv()
            add_block(block(t, 1 - y, x))
            gp_copy(1, t, y, True).wait_recv()
            add_block(block(t, y, 1 - x))
            gp_copy(0, t, 1 - x, True).wait_recv()
            gp_copy(1, t, 1 - y, True).wait_recv()
            add_block(block(t, 1 - y, 1 - x))
            return carry

        lax.fori_loop(0, line, last_step, 0)
        mixer(r)
        lax.fori_loop(0, line, settle_gather, 0)
        pl.when(r == 0)(lambda: w_in_copy.wait())
        def product(b):
            w_rows = pl.ds(pl.multiple_of(b * width, width), width)
            value = lax.dot_general(proj_ref[r, 0], w_in_ref[0, w_rows, :], NT, preferred_element_type=jnp.float32)
            for i in range(1, 3):
                value += lax.dot_general(proj_ref[r, i], w_in_ref[i, w_rows, :], NT, preferred_element_type=jnp.float32)
            part[b] = value.astype(part.dtype)

        def first_step(k, carry):
            t = far_first(k)
            product(block(t, 1 - y, 1 - x))
            p_copy(0, t, 1 - x).start()
            p_copy(1, t, 1 - y).start()
            product(block(t, 1 - y, x))
            p_copy(0, t, x).start()
            product(block(t, y, 1 - x))
            p_copy(1, t, y).start()
            product(block(t, y, x))
            return carry

        lax.fori_loop(0, line, first_step, 0)

        def second_step(k, carry):
            t = far_first(k)
            for half in range(2):
                p, q, p_dev, q_dev, at = sides(half)
                p_copy(half, t, 1 - q).wait_recv()
                b = at(t, p, 1 - q)
                value = part[b, rows(half)].astype(jnp.float32) + got_p[half, t * 2 + 1 - q].astype(jnp.float32)
                part[b, rows(half)] = value.astype(part.dtype)
                q_copy(half, t).start()
            long_taps_grad(k)
            return carry

        lax.fori_loop(0, line, second_step, 0)
        short_taps_grad()

        def third_step(k, carry):
            t = far_first(k)
            for half in range(2):
                p, q, p_dev, q_dev, at = sides(half)
                p_copy(half, t, q).wait_recv()
                q_copy(half, t).wait_recv()
                b = block(t, y, x)
                total_ref = sum_ref.at[half]
                total_ref[...] = (
                    part[b, rows(half)].astype(jnp.float32)
                    + got_p[half, t * 2 + q].astype(jnp.float32)
                    + got_q[half, t].astype(jnp.float32)
                )

                @pl.when(jnp.logical_and(t >= a, not_bottom))
                def _():
                    up_copy(half, t).wait_recv()
                    total_ref[...] += got_up[half, t].astype(jnp.float32)

                @pl.when(jnp.logical_and(t <= a, not_top))
                def _():
                    down_copy(half, t).wait_recv()
                    total_ref[...] += got_down[half, t].astype(jnp.float32)

                part[b, rows(half)] = total_ref[...].astype(part.dtype)
                pl.when(t > a)(lambda: up_copy(half, t).start())
                pl.when(t < a)(lambda: down_copy(half, t).start())
                pl.when(t == a)(lambda: turn_copy(half, r).start())
            return carry

        lax.fori_loop(0, line, third_step, 0)

        return round_carry

    lax.fori_loop(0, rounds, one_round, 0)
    settle_sum(rounds - 1)
    for ct in range(tiles):
        long_out[:, lanes(ct)] = long_part[ct].sum(axis=1)
        for i in range(3):
            short_out[i, :, lanes(ct)] = short_part[i, :, ct].sum(axis=1)
    for half in range(2):
        turn_copy(half, rounds - 1).wait_recv()
    result_ref[...] = turned[rounds - 1]


def local(upstream, projected, w_in, w_out, short_filter, long_filter):
    rounds = projected.shape[1]
    group = lax.axis_size("group")
    sections = lax.axis_size("section")
    line = group // 4
    _, tokens, width = upstream.shape
    model_width, parts, local_ch = w_in.shape[1:]
    short_extent = short_filter.shape[2]
    extent = long_filter.shape[1]
    tiles = local_ch // LANES
    half_rows = tokens // 2
    dma = pltpu.SemaphoreType.DMA
    vmem16 = lambda *shape: pltpu.VMEM(shape, jnp.bfloat16)
    vmem32 = lambda *shape: pltpu.VMEM(shape, jnp.float32)
    scratch = [
        vmem16(parts, model_width, local_ch),
        vmem16(local_ch, model_width),
        dma((2,)),
        vmem16(group, tokens, width),
        vmem16(2, 2 * line, half_rows, width),
        vmem16(2, line, half_rows, width),
        vmem16(2, line, half_rows, width),
        vmem16(2, line, half_rows, width),
        vmem32(2, half_rows, width),
        vmem16(rounds + 1, tokens, width),
        vmem16(group, tokens, width),
        vmem32(tokens, local_ch),
        vmem32(parts, tiles, PAD + tokens, LANES),
        vmem32(parts, tiles, tokens, LANES),
        vmem32(tiles, extent + tokens, LANES),
        vmem32(tiles, tokens, LANES),
        vmem32(tiles, tokens + extent, LANES),
        vmem32(parts, tiles, tokens + PAD, LANES),
        vmem32(tiles, extent, 8, LANES),
        vmem32(parts, short_extent, tiles, 8, LANES),
    ]
    scratch += [dma((2, 2 * line))] * 2 + [dma((2, line))] * 6 + [dma((2, rounds))] * 2
    scratch += [dma((2, line))] * 5 + [dma((2, 2 * line))] * 2
    vmem = pl.BlockSpec(memory_space=pltpu.VMEM)
    hbm = pl.BlockSpec(memory_space=pl.ANY)
    input_grad, proj_grad, long_grad, short_grad = pl.pallas_call(
        functools.partial(mixers_body, line, sections),
        out_shape=(
            jax.ShapeDtypeStruct((tokens, width), jnp.bfloat16),
            jax.ShapeDtypeStruct((rounds, parts, tokens, local_ch), jnp.bfloat16),
            jax.ShapeDtypeStruct((extent, local_ch), jnp.float32),
            jax.ShapeDtypeStruct((parts, short_extent, local_ch), jnp.float32),
        ),
        in_specs=[vmem, vmem, hbm, hbm, vmem, vmem],
        out_specs=(vmem,) * 4,
        scratch_shapes=scratch,
        compiler_params=pltpu.CompilerParams(
            collective_id=0, has_side_effects=True, vmem_limit_bytes=56 * 2**20
        ),
        name="mixers",
    )(
        upstream[0],
        projected[0].transpose(0, 2, 1, 3),
        w_in[0].transpose(1, 0, 2),
        w_out[0],
        short_filter[0],
        long_filter[0],
    )
    return (input_grad[None], proj_grad.transpose(0, 2, 1, 3)[None], long_grad[None], short_grad[None])


def solution(mesh):
    in_specs = (
        P("section", None, "group"),
        P("section", None, None, None, "group"),
        P("section", None, None, "group"),
        P("section", "group", None),
        P("section", None, None, "group"),
        P("section", None, "group"),
    )
    out_specs = (
        P("section", None, "group"),
        P("section", None, None, None, "group"),
        P("section", None, "group"),
        P("section", None, None, "group"),
    )
    return jax.shard_map(local, mesh=mesh, in_specs=in_specs, out_specs=out_specs, check_vma=False)
```

```python
import functools

import jax
import jax.numpy as jnp
from jax import lax
from jax.experimental import pallas as pl
from jax.experimental.pallas import tpu as pltpu
from jax.sharding import PartitionSpec as P

NT = (((1,), (1,)), ((), ()))


LANES = 128
PAD = 8


def mixers_body(
    line,
    sections,
    first_ref,
    projected_ref,
    w_in_any,
    w_out_any,
    short_ref,
    long_ref,
    result_ref,
    proj_ref,
    long_out,
    short_out,
    w_in_ref,
    w_out_ref,
    weight_sems,
    part,
    got_p,
    got_q,
    got_up,
    got_down,
    sum_ref,
    turned,
    landed,
    total,
    signal,
    conv,
    gating,
    mixed,
    mixed_grad,
    grads,
    long_part,
    short_part,
    p_send,
    p_recv,
    q_send,
    q_recv,
    up_send,
    up_recv,
    down_send,
    down_recv,
    turn_send,
    turn_recv,
    gl_up,
    gl_down,
    gl_recv,
    gq_send,
    gq_recv,
    gp_send,
    gp_recv,
):
    rounds = projected_ref.shape[0]
    tokens = landed.shape[1]
    tiles = conv.shape[1]
    extent = long_ref.shape[0]
    short_extent = short_ref.shape[1]
    chunk = extent // line
    strip = min(tokens, 128)
    w_out_copy = pltpu.make_async_copy(w_out_any, w_out_ref, weight_sems.at[0])
    w_in_copy = pltpu.make_async_copy(w_in_any, w_in_ref, weight_sems.at[1])
    w_out_copy.start()
    w_in_copy.start()
    section = lax.axis_index("section")
    me = lax.axis_index("group")
    a = me // 4
    y = (me // 2) % 2
    x = me % 2
    half_rows = landed.shape[1] // 2

    def block(t, yy, xx):
        return t * 4 + yy * 2 + xx

    to_x = {"group": block(a, y, 1 - x)}
    to_y = {"group": block(a, 1 - y, x)}
    above = {"group": lax.rem(me + 4, 4 * line)}
    below = {"group": lax.rem(me + 4 * line - 4, 4 * line)}
    to_section = {"section": lax.rem(section + sections - 1, sections)}
    from_section = {"section": lax.rem(section + 1, sections)}
    not_top = a < line - 1
    not_bottom = a > 0

    barrier = pltpu.get_barrier_semaphore()

    def greet(device):
        pl.semaphore_signal(barrier, inc=1, device_id=device, device_id_type=pl.DeviceIdType.MESH)

    greet(to_x)
    greet(to_y)
    pl.when(not_top)(lambda: greet(above))
    pl.when(not_bottom)(lambda: greet(below))
    greet(from_section)
    ends = 2 + jnp.where(not_top, 1, 0) + jnp.where(not_bottom, 1, 0)
    pl.semaphore_wait(barrier, ends + 1)

    def far_first(k):
        low = line - 1 - k
        low = jnp.where(low <= a, low - 1, low)
        high = jnp.where(k >= a, k + 1, k)
        other = jnp.where(a < line // 2, low, high)
        return jnp.where(k == line - 1, a, other)

    def near_first(k):
        return far_first(line - 1 - k)

    def rows(half):
        return pl.ds(half * half_rows, half_rows)

    def copy(source, target, send, recv, device):
        return pltpu.make_async_remote_copy(
            src_ref=source,
            dst_ref=target,
            send_sem=send,
            recv_sem=recv,
            device_id=device,
            device_id_type=pl.DeviceIdType.MESH,
        )

    def sides(half):
        if half == 0:
            return y, x, to_y, to_x, lambda t, pp, qq: block(t, pp, qq)
        return x, y, to_x, to_y, lambda t, pp, qq: block(t, qq, pp)

    width = part.shape[2]

    def p_copy(half, t, qq):
        p, q, p_dev, q_dev, at = sides(half)
        slot = t * 2 + qq
        return copy(
            part.at[at(t, 1 - p, qq), rows(half)],
            got_p.at[half, slot],
            p_send.at[half, slot],
            p_recv.at[half, slot],
            p_dev,
        )

    def q_copy(half, t):
        p, q, p_dev, q_dev, at = sides(half)
        return copy(
            part.at[at(t, p, 1 - q), rows(half)],
            got_q.at[half, t],
            q_send.at[half, t],
            q_recv.at[half, t],
            q_dev,
        )

    def up_copy(half, t):
        return copy(
            part.at[block(t, y, x), rows(half)], got_up.at[half, t], up_send.at[half, t], up_recv.at[half, t], above
        )

    def down_copy(half, t):
        return copy(
            part.at[block(t, y, x), rows(half)],
            got_down.at[half, t],
            down_send.at[half, t],
            down_recv.at[half, t],
            below,
        )

    def turn_copy(half, r):
        return copy(
            part.at[me, rows(half)], turned.at[r, rows(half)], turn_send.at[half, r], turn_recv.at[half, r], to_section
        )

    depth = landed.shape[2]

    def gl_copy(half, t, send, device):
        piece = landed.at[block(t, y, x), rows(half)]
        return copy(piece, piece, send.at[half, t], gl_recv.at[half, t], device)

    def gq_copy(half, t, arriving):
        p, q, p_dev, q_dev, at = sides(half)
        piece = landed.at[at(t, p, 1 - q if arriving else q), rows(half)]
        return copy(piece, piece, gq_send.at[half, t], gq_recv.at[half, t], q_dev)

    def gp_copy(half, t, qq, arriving):
        p, q, p_dev, q_dev, at = sides(half)
        piece = landed.at[at(t, 1 - p if arriving else p, qq), rows(half)]
        slot = t * 2 + qq
        return copy(piece, piece, gp_send.at[half, slot], gp_recv.at[half, slot], p_dev)

    def add_block(b):
        columns = pl.ds(pl.multiple_of(b * depth, depth), depth)
        total[...] += lax.dot_general(landed[b], w_out_ref[:, columns], NT, preferred_element_type=jnp.float32)


    def lanes(ct):
        return slice(ct * LANES, (ct + 1) * LANES)

    def short_convs(r):
        for ct in range(tiles):
            for i in range(3):
                signal[i, ct, PAD:] = projected_ref[r, i, :, lanes(ct)].astype(jnp.float32)
                value = short_ref[i, 0:1, lanes(ct)] * signal[i, ct, PAD:]
                for j in range(1, short_extent):
                    value += short_ref[i, j : j + 1, lanes(ct)] * signal[i, ct, PAD - j : PAD - j + tokens]
                conv[i, ct] = value
            gating[ct, extent:] = conv[1, ct] * conv[2, ct]
            mixed[ct] = jnp.zeros((tokens, LANES), jnp.float32)

    def tap_sum(source, ct, base, step, first, count, start):
        def eight(n, running):
            base_tap = pl.multiple_of(first + n * 8, 8)
            weights = long_ref[pl.ds(base_tap, 8), lanes(ct)]
            for jj in range(8):
                j = base_tap + jj
                running += weights[jj : jj + 1] * source[ct, pl.ds(base + step * j, strip)]
            return running

        return lax.fori_loop(0, count // 8, eight, start)

    def long_conv(k):
        for ct in range(tiles):
            for t0 in range(0, tokens, strip):
                mixed[ct, t0 : t0 + strip] = tap_sum(
                    gating, ct, extent + t0, -1, k * chunk, chunk, mixed[ct, t0 : t0 + strip]
                )

    def folded(value):
        return value.reshape(value.shape[0] // 8, 8, LANES).sum(axis=0)

    def long_taps_grad(k):
        for ct in range(tiles):
            for t0 in range(0, tokens, strip):
                fixed = mixed_grad[ct, t0 : t0 + strip]

                def four(n, carry):
                    for jj in range(4):
                        j = k * chunk + n * 4 + jj
                        long_part[ct, j] += folded(fixed * gating[ct, pl.ds(extent + t0 - j, strip)])
                    return carry

                lax.fori_loop(0, chunk // 4, four, 0)

    def short_taps_grad():
        for ct in range(tiles):
            for i in range(3):
                for j in range(short_extent):
                    short_part[i, j, ct] += folded(grads[i, ct, :tokens] * signal[i, ct, PAD - j : PAD - j + tokens])

    def mixer(r):
        for ct in range(tiles):
            out_grad = total[:, lanes(ct)]
            mixed_grad[ct, :tokens] = out_grad * conv[0, ct]
            grads[0, ct, :tokens] = out_grad * mixed[ct]
        for ct in range(tiles):
            for t0 in range(0, tokens, strip):
                span = slice(t0, t0 + strip)
                gating_grad = tap_sum(mixed_grad, ct, t0, 1, 0, extent, jnp.zeros((strip, LANES), jnp.float32))
                grads[1, ct, span] = gating_grad * conv[2, ct, span]
                grads[2, ct, span] = gating_grad * conv[1, ct, span]
        for ct in range(tiles):
            for i in range(3):
                value = short_ref[i, 0:1, lanes(ct)] * grads[i, ct, :tokens]
                for j in range(1, short_extent):
                    value += short_ref[i, j : j + 1, lanes(ct)] * grads[i, ct, j : j + tokens]
                proj_ref[r, i, :, lanes(ct)] = value.astype(proj_ref.dtype)

    signal[...] = jnp.zeros_like(signal)
    gating[...] = jnp.zeros_like(gating)
    mixed_grad[...] = jnp.zeros_like(mixed_grad)
    grads[...] = jnp.zeros_like(grads)
    long_part[...] = jnp.zeros_like(long_part)
    short_part[...] = jnp.zeros_like(short_part)
    turned[rounds] = first_ref[...]

    def settle_sum(r):
        def settle(t, carry):
            for half in range(2):
                for qq in range(2):
                    p_copy(half, t, qq).wait_send()
                q_copy(half, t).wait_send()
                pl.when(t > a)(lambda: up_copy(half, t).wait_send())
                pl.when(t < a)(lambda: down_copy(half, t).wait_send())
            return carry

        lax.fori_loop(0, line, settle, 0)
        for half in range(2):
            turn_copy(half, r).wait_send()

    def settle_gather(t, carry):
        for half in range(2):
            pl.when(jnp.logical_and(t <= a, not_top))(lambda: gl_copy(half, t, gl_up, above).wait_send())
            pl.when(jnp.logical_and(t >= a, not_bottom))(lambda: gl_copy(half, t, gl_down, below).wait_send())
            gq_copy(half, t, False).wait_send()
            for qq in range(2):
                gp_copy(half, t, qq, False).wait_send()
        return carry

    def one_round(r, round_carry):
        total[...] = jnp.zeros_like(total)

        def line_step(k, carry):
            t = near_first(k)
            for half in range(2):
                p, q, p_dev, q_dev, at = sides(half)

                @pl.when(t == a)
                def _():
                    pl.when(r > 0)(lambda: turn_copy(half, r - 1).wait_recv())
                    landed[me, rows(half)] = turned[jnp.where(r > 0, r - 1, rounds), rows(half)]

                pl.when(t != a)(lambda: gl_copy(half, t, gl_up, above).wait_recv())
                pl.when(jnp.logical_and(t <= a, not_top))(lambda: gl_copy(half, t, gl_up, above).start())
                pl.when(jnp.logical_and(t >= a, not_bottom))(lambda: gl_copy(half, t, gl_down, below).start())
                gq_copy(half, t, False).start()
                gp_copy(half, t, q, False).start()

            @pl.when(k == 0)
            def _():
                pl.when(r == 0)(lambda: w_out_copy.wait())
                short_convs(r)

            add_block(block(t, y, x))
            return carry

        lax.fori_loop(0, line, line_step, 0)
        pl.when(r > 0)(lambda: settle_sum(r - 1))

        def pass_step(k, carry):
            t = near_first(k)
            for half in range(2):
                p, q, p_dev, q_dev, at = sides(half)
                gq_copy(half, t, True).wait_recv()
                gp_copy(half, t, 1 - q, False).start()
            long_conv(k)
            return carry

        lax.fori_loop(0, line, pass_step, 0)

        def last_step(k, carry):
            t = near_first(k)
            gp_copy(0, t, x, True).wait_recv()
            add_block(block(t, 1 - y, x))
            gp_copy(1, t, y, True).wait_recv()
            add_block(block(t, y, 1 - x))
            gp_copy(0, t, 1 - x, True).wait_recv()
            gp_copy(1, t, 1 - y, True).wait_recv()
            add_block(block(t, 1 - y, 1 - x))
            return carry

        lax.fori_loop(0, line, last_step, 0)
        mixer(r)
        lax.fori_loop(0, line, settle_gather, 0)
        pl.when(r == 0)(lambda: w_in_copy.wait())
        def product(b):
            w_rows = pl.ds(pl.multiple_of(b * width, width), width)
            value = lax.dot_general(proj_ref[r, 0], w_in_ref[0, w_rows, :], NT, preferred_element_type=jnp.float32)
            for i in range(1, 3):
                value += lax.dot_general(proj_ref[r, i], w_in_ref[i, w_rows, :], NT, preferred_element_type=jnp.float32)
            part[b] = value.astype(part.dtype)

        def first_step(k):
            t = far_first(k)
            product(block(t, 1 - y, 1 - x))
            p_copy(0, t, 1 - x).start()
            p_copy(1, t, 1 - y).start()
            product(block(t, 1 - y, x))
            p_copy(0, t, x).start()
            product(block(t, y, 1 - x))
            p_copy(1, t, y).start()
            product(block(t, y, x))


        def second_step(k):
            t = far_first(k)
            for half in range(2):
                p, q, p_dev, q_dev, at = sides(half)
                p_copy(half, t, 1 - q).wait_recv()
                b = at(t, p, 1 - q)
                value = part[b, rows(half)].astype(jnp.float32) + got_p[half, t * 2 + 1 - q].astype(jnp.float32)
                part[b, rows(half)] = value.astype(part.dtype)
                q_copy(half, t).start()
            long_taps_grad(k)
            pl.when(k == line - 1)(short_taps_grad)


        def third_step(k):
            t = far_first(k)
            for half in range(2):
                p, q, p_dev, q_dev, at = sides(half)
                p_copy(half, t, q).wait_recv()
                q_copy(half, t).wait_recv()
                b = block(t, y, x)
                total_ref = sum_ref.at[half]
                total_ref[...] = (
                    part[b, rows(half)].astype(jnp.float32)
                    + got_p[half, t * 2 + q].astype(jnp.float32)
                    + got_q[half, t].astype(jnp.float32)
                )

                @pl.when(jnp.logical_and(t >= a, not_bottom))
                def _():
                    up_copy(half, t).wait_recv()
                    total_ref[...] += got_up[half, t].astype(jnp.float32)

                @pl.when(jnp.logical_and(t <= a, not_top))
                def _():
                    down_copy(half, t).wait_recv()
                    total_ref[...] += got_down[half, t].astype(jnp.float32)

                part[b, rows(half)] = total_ref[...].astype(part.dtype)
                pl.when(t > a)(lambda: up_copy(half, t).start())
                pl.when(t < a)(lambda: down_copy(half, t).start())
                pl.when(t == a)(lambda: turn_copy(half, r).start())

        def staggered(k, carry):
            pl.when(k < line)(lambda: first_step(k))
            pl.when(jnp.logical_and(k >= 1, k <= line))(lambda: second_step(k - 1))
            pl.when(k >= 2)(lambda: third_step(k - 2))
            return carry

        lax.fori_loop(0, line + 2, staggered, 0)

        return round_carry

    lax.fori_loop(0, rounds, one_round, 0)
    settle_sum(rounds - 1)
    for ct in range(tiles):
        long_out[:, lanes(ct)] = long_part[ct].sum(axis=1)
        for i in range(3):
            short_out[i, :, lanes(ct)] = short_part[i, :, ct].sum(axis=1)
    for half in range(2):
        turn_copy(half, rounds - 1).wait_recv()
    result_ref[...] = turned[rounds - 1]


def local(upstream, projected, w_in, w_out, short_filter, long_filter):
    rounds = projected.shape[1]
    group = lax.axis_size("group")
    sections = lax.axis_size("section")
    line = group // 4
    _, tokens, width = upstream.shape
    model_width, parts, local_ch = w_in.shape[1:]
    short_extent = short_filter.shape[2]
    extent = long_filter.shape[1]
    tiles = local_ch // LANES
    half_rows = tokens // 2
    dma = pltpu.SemaphoreType.DMA
    vmem16 = lambda *shape: pltpu.VMEM(shape, jnp.bfloat16)
    vmem32 = lambda *shape: pltpu.VMEM(shape, jnp.float32)
    scratch = [
        vmem16(parts, model_width, local_ch),
        vmem16(local_ch, model_width),
        dma((2,)),
        vmem16(group, tokens, width),
        vmem16(2, 2 * line, half_rows, width),
        vmem16(2, line, half_rows, width),
        vmem16(2, line, half_rows, width),
        vmem16(2, line, half_rows, width),
        vmem32(2, half_rows, width),
        vmem16(rounds + 1, tokens, width),
        vmem16(group, tokens, width),
        vmem32(tokens, local_ch),
        vmem32(parts, tiles, PAD + tokens, LANES),
        vmem32(parts, tiles, tokens, LANES),
        vmem32(tiles, extent + tokens, LANES),
        vmem32(tiles, tokens, LANES),
        vmem32(tiles, tokens + extent, LANES),
        vmem32(parts, tiles, tokens + PAD, LANES),
        vmem32(tiles, extent, 8, LANES),
        vmem32(parts, short_extent, tiles, 8, LANES),
    ]
    scratch += [dma((2, 2 * line))] * 2 + [dma((2, line))] * 6 + [dma((2, rounds))] * 2
    scratch += [dma((2, line))] * 5 + [dma((2, 2 * line))] * 2
    vmem = pl.BlockSpec(memory_space=pltpu.VMEM)
    hbm = pl.BlockSpec(memory_space=pl.ANY)
    input_grad, proj_grad, long_grad, short_grad = pl.pallas_call(
        functools.partial(mixers_body, line, sections),
        out_shape=(
            jax.ShapeDtypeStruct((tokens, width), jnp.bfloat16),
            jax.ShapeDtypeStruct((rounds, parts, tokens, local_ch), jnp.bfloat16),
            jax.ShapeDtypeStruct((extent, local_ch), jnp.float32),
            jax.ShapeDtypeStruct((parts, short_extent, local_ch), jnp.float32),
        ),
        in_specs=[vmem, vmem, hbm, hbm, vmem, vmem],
        out_specs=(vmem,) * 4,
        scratch_shapes=scratch,
        compiler_params=pltpu.CompilerParams(
            collective_id=0, has_side_effects=True, vmem_limit_bytes=56 * 2**20
        ),
        name="mixers",
    )(
        upstream[0],
        projected[0].transpose(0, 2, 1, 3),
        w_in[0].transpose(1, 0, 2),
        w_out[0],
        short_filter[0],
        long_filter[0],
    )
    return (input_grad[None], proj_grad.transpose(0, 2, 1, 3)[None], long_grad[None], short_grad[None])


def solution(mesh):
    in_specs = (
        P("section", None, "group"),
        P("section", None, None, None, "group"),
        P("section", None, None, "group"),
        P("section", "group", None),
        P("section", None, None, "group"),
        P("section", None, "group"),
    )
    out_specs = (
        P("section", None, "group"),
        P("section", None, None, None, "group"),
        P("section", None, "group"),
        P("section", None, None, "group"),
    )
    return jax.shard_map(local, mesh=mesh, in_specs=in_specs, out_specs=out_specs, check_vma=False)
```
